256 devices in a mesh: seq: 64 (over x, z, y_lo), ch: 4 (over y_hi, core).
Axes of the slice: x: 4, y: 4 (y_hi: 2, y_lo: 2; y = y_hi * 2 + y_lo), z: 8, core: 2. Of those that a mesh axis runs over, the one named last changes fastest.
Arguments:
- grad_output: bfloat16 [8192, 16, 512], P('seq', 'ch'), may hold values from -6 to 6
- query_act: bfloat16 [8192, 16, 512], P('seq', 'ch'), may hold values from -6 to 6
- key_act: bfloat16 [8192, 16, 512], P('seq', 'ch'), may hold values from -6 to 6
- value_act: bfloat16 [8192, 16, 512], P('seq', 'ch'), may hold values from -6 to 6
- long_filter: bfloat16 [8192, 512], P('seq'), may hold values from -0.0625 to 0.0625
Outputs:
- input_grad: bfloat16 [3, 8192, 16, 512], P(None, 'seq', 'ch')
- filter_grad: float32 [8192, 512], P('seq', 'ch')
The draws below stay inside these ranges and needn't reach their ends.
All inputs are finite; a program needn't handle non-finite values.
Results may differ from the reference program's by a relative error of at most 0.0049.
Values may be sent and summed in bfloat16 or wider, within the bound.
A program may use at most 128 MiB of HBM per device.

```python
import math
import jax
import jax.numpy as jnp
from jax import lax

G = 512
MEMBERS = 16
TOKENS = 8192


def shard_levels(rng, dims, split, smallest, largest):
    gain, own = 1.0, jax.random.fold_in(rng, 6)
    for position, shards_of in split:
        steps = jnp.exp(jax.random.uniform(jax.random.fold_in(own, position), (shards_of,), jnp.float32, smallest / len(split), largest / len(split)))
        gain = gain * jnp.repeat(steps, dims[position] // shards_of).reshape([-1 if axis == position else 1 for axis in range(len(dims))])
    return gain


def normal_values(own_key, shape, spread, bound, split=(), kind=jnp.bfloat16):
    result = spread * jax.random.normal(own_key, shape, jnp.float32)
    if split:
        result = result * shard_levels(own_key, shape, split, -0.22, 0.18)
    return jnp.clip(result, -bound, bound).astype(kind)


def setup_inputs(seed: int = 0) -> dict:
    key_list = jax.random.split(jax.random.key(seed), 6)
    grad_output = normal_values(key_list[0], (TOKENS, MEMBERS, G), 1.0, 6.0, ((0, 64), (1, 4)))
    query_act = normal_values(key_list[1], (TOKENS, MEMBERS, G), 1.0, 6.0, ((0, 64), (1, 4)))
    key_act = normal_values(key_list[2], (TOKENS, MEMBERS, G), 1.0, 6.0, ((0, 64), (1, 4)))
    value_act = normal_values(key_list[3], (TOKENS, MEMBERS, G), 1.0, 6.0, ((0, 64), (1, 4)))
    long_filter = normal_values(key_list[4], (TOKENS, G), TOKENS ** -0.5, 0.0625, ((0, 64),))
    return {"grad_output": grad_output, "query_act": query_act, "key_act": key_act, "value_act": value_act, "long_filter": long_filter}


def one_block(block):
    grad_block, query_block, key_block, value_block, filter_block = block
    length = grad_block.shape[0]
    padded = 2 * length
    gated_grad = (grad_block.astype(jnp.float32) * query_block.astype(jnp.float32)).astype(jnp.bfloat16)
    mixed_input = (key_block.astype(jnp.float32) * value_block.astype(jnp.float32)).astype(jnp.bfloat16)
    spec_gated = jnp.fft.rfft(gated_grad.astype(jnp.float32), n=padded, axis=0)
    spec_mixed = jnp.fft.rfft(mixed_input.astype(jnp.float32), n=padded, axis=0)
    spec_long = jnp.fft.rfft(filter_block.astype(jnp.float32), n=padded, axis=0)[:, None, :]
    conv_out = jnp.fft.irfft(spec_long * spec_mixed, n=padded, axis=0)[:length].astype(jnp.float32)
    mixed_grad = jnp.fft.irfft(jnp.conj(spec_long) * spec_gated, n=padded, axis=0)[:length].astype(jnp.float32)
    lag_spec = lax.optimization_barrier(jnp.sum(spec_gated * jnp.conj(spec_mixed), axis=1))
    lag_grad = jnp.fft.irfft(lag_spec, n=padded, axis=0)[:length].astype(jnp.float32)
    query_grad = (grad_block.astype(jnp.float32) * conv_out).astype(jnp.bfloat16)
    key_grad = (mixed_grad * value_block.astype(jnp.float32)).astype(jnp.bfloat16)
    value_grad = (mixed_grad * key_block.astype(jnp.float32)).astype(jnp.bfloat16)
    return (jnp.stack([query_grad, key_grad, value_grad]), lag_grad)

def reference(grad_output, query_act, key_act, value_act, long_filter):
    block_width = min(G, 64)
    block_count = G // block_width

    def regroup(array):
        return jnp.transpose(array.reshape(TOKENS, MEMBERS, block_count, block_width), (2, 0, 1, 3))
    filter_blocks = jnp.transpose(long_filter.reshape(TOKENS, block_count, block_width), (1, 0, 2))
    grads, lags = lax.map(one_block, (regroup(grad_output), regroup(query_act), regroup(key_act), regroup(value_act), filter_blocks))
    input_grad = jnp.transpose(grads, (1, 2, 3, 0, 4)).reshape(3, TOKENS, MEMBERS, G)
    lag_grad = jnp.transpose(lags, (1, 0, 2)).reshape(TOKENS, G)
    filter_grad = lag_grad * (1.0 / math.sqrt(MEMBERS * TOKENS))
    return (input_grad, filter_grad)
```

```python
import math

import jax
import jax.numpy as jnp
from jax import lax
from jax.experimental import pallas as pl
from jax.experimental.pallas import tpu as pltpu
from jax.sharding import PartitionSpec as P

F32 = jnp.float32
BF16 = jnp.bfloat16

SEQ = 64
CH = 4
DEVICES = SEQ * CH
BLOCK = 128
MEMBERS = 16
OWN = 4
GROUPS = 512
TILES = GROUPS // 128
PAIR = 2 * BLOCK
STEPS = SEQ // 2
ROWS = STEPS * MEMBERS
SCALE = 1.0 / math.sqrt(MEMBERS * SEQ * BLOCK)


def dot_rows(left, right):
    return lax.dot_general(
        left, right, (((1,), (1,)), ((), ())), preferred_element_type=F32
    )


def dot(left, right):
    return jnp.dot(left, right, preferred_element_type=F32)


def products(left, right, rows):
    def body(k, carry):
        at = pl.ds(pl.multiple_of(16 * k, 16), 16)
        value = (left[at].astype(F32) * right[at].astype(F32)).astype(BF16).astype(F32)
        value = value.reshape(64, GROUPS)
        for tile in range(TILES):
            rows[tile, pl.ds(pl.multiple_of(64 * k, 64), 64), :] = value[
                :, 128 * tile : 128 * tile + 128
            ]
        return carry

    lax.fori_loop(0, BLOCK // 16, body, 0)


def spread(mixed_rows, gated_rows, tile, turned, send):
    for arr, rows in enumerate((mixed_rows, gated_rows)):
        for m in range(OWN):
            part = rows.at[tile][pl.ds(m, BLOCK, stride=OWN), :]
            turned[pl.ds(arr * OWN + m, 128, stride=8), :] = part.T
    low = 2 * (tile % 2)
    send[tile // 2, low : low + 2] = turned[...].reshape(2, SEQ, 8, BLOCK).astype(BF16)


def collect(recv, tile, turned, conv_rows, back_rows):
    low = 2 * (tile % 2)
    turned[...] = recv[tile // 2, low : low + 2].astype(F32).reshape(1024, BLOCK)
    for arr, rows in enumerate((conv_rows, back_rows)):
        for m in range(OWN):
            part = turned[pl.ds(arr * OWN + m, 128, stride=8), :]
            rows.at[tile][pl.ds(m, BLOCK, stride=OWN), :] = part.T


def gradients(tile, conv_rows, back_rows, grad, key, value, out):
    lanes = pl.ds(128 * tile, 128)

    def body(k, carry):
        at = pl.ds(pl.multiple_of(16 * k, 16), 16)
        rows = pl.ds(pl.multiple_of(64 * k, 64), 64)
        conv = conv_rows[tile, rows, :].reshape(16, OWN, 128)
        back = back_rows[tile, rows, :].reshape(16, OWN, 128)
        out[0, at, :, lanes] = (grad[at, :, lanes].astype(F32) * conv).astype(BF16)
        out[1, at, :, lanes] = (back * value[at, :, lanes].astype(F32)).astype(BF16)
        out[2, at, :, lanes] = (back * key[at, :, lanes].astype(F32)).astype(BF16)
        return carry

    lax.fori_loop(0, BLOCK // 16, body, 0)


def toeplitz(taps, half, strip):
    strip[half, :, 0:128] = jnp.zeros((128, 128), BF16)

    def body(t, carry):
        now = taps[half, pl.ds(t, 1), :]
        before = taps[half, pl.ds(jnp.maximum(t - 1, 0), 1), :] * jnp.where(t > 0, 1.0, 0.0)
        both = jnp.broadcast_to(jnp.concatenate([before, now], axis=1), (128, 256))
        skewed = pltpu.roll(both, 0, 1, stride=1, stride_axis=0)
        at = pl.ds(pl.multiple_of(128 * (t + 1), 128), 128)
        strip[half, :, at] = skewed[:, 128:].astype(BF16)
        return carry

    lax.fori_loop(0, SEQ, body, 0, unroll=8)


def unpack(recv, half, mixed, gated):
    def body(j, carry):
        rows = pl.ds(pl.multiple_of(MEMBERS * j, MEMBERS), MEMBERS)
        for h in range(2):
            inputs, gates = [], []
            for c in (0, 2):
                low = recv[half, c, 2 * j + h].astype(F32)
                high = recv[half, c + 1, 2 * j + h].astype(F32)
                inputs.append(jnp.concatenate([low[:OWN], high[:OWN]], axis=0))
                gates.append(jnp.concatenate([low[OWN:], high[OWN:]], axis=0))
            lanes = slice(128 * h, 128 * h + 128)
            mixed[rows, lanes] = jnp.concatenate(inputs, axis=0).astype(BF16)
            gated[rows, lanes] = jnp.concatenate(gates, axis=0).astype(BF16)
        return carry

    lax.fori_loop(0, STEPS, body, 0, unroll=4)


def pack(conv, back, half, send):
    def body(i, carry):
        for h in range(2):
            lanes = slice(128 * h, 128 * h + 128)
            for c in (0, 2):
                rows = pl.ds(pl.multiple_of(MEMBERS * i + OWN * c, 8), 8)
                y = conv[rows, lanes]
                m = back[rows, lanes]
                send[half, c, 2 * i + h] = jnp.concatenate([y[:OWN], m[:OWN]], axis=0).astype(BF16)
                send[half, c + 1, 2 * i + h] = jnp.concatenate([y[OWN:], m[OWN:]], axis=0).astype(BF16)
        return carry

    lax.fori_loop(0, STEPS, body, 0, unroll=4)


def convolve(strip, half, mixed, gated, conv, back):
    for d in range(STEPS):
        o = PAIR * d
        weights = jnp.concatenate(
            [strip[half, :, o + 128 : o + 384], strip[half, :, o : o + 256]], axis=0
        )
        skip = MEMBERS * d
        y = dot(mixed[0 : ROWS - skip, :], weights)
        m = dot_rows(gated[skip:ROWS, :], weights)
        if d == 0:
            conv[...] = y
            back[...] = m
        else:
            conv[skip:ROWS, :] += y
            back[0 : ROWS - skip, :] += m


def lag(mixed, gated, half, flipped, outer, lags):
    row = lax.broadcasted_iota(jnp.int32, (PAIR, PAIR), 0)
    column = lax.broadcasted_iota(jnp.int32, (PAIR, PAIR), 1)
    eye = jnp.where(row == column, 1.0, 0.0).astype(BF16)
    flipped[...] = dot_rows(eye, mixed[...]).astype(BF16)
    outer[:, SEQ * BLOCK :] = jnp.zeros((PAIR, 256), F32)
    gated[ROWS:, :] = jnp.zeros((ROWS, PAIR), BF16)
    for d in range(STEPS):
        depth = ROWS if d < STEPS // 2 else ROWS // 2
        skip = MEMBERS * d
        outer[:, PAIR * d : PAIR * d + PAIR] = dot(
            flipped[:, :depth], gated[skip : skip + depth, :]
        )
    wide = 1024 + 128

    def chunk(n, carry):
        base = pl.multiple_of(1024 * n, 128)
        after = pl.multiple_of(base + 128, 128)

        def part(q):
            first = outer[8 * q : 8 * q + 8, pl.ds(base, wide)]
            return first + outer[128 + 8 * q : 136 + 8 * q, pl.ds(after, wide)]

        total = part(0)
        for q in range(1, 16):
            total = total + pltpu.roll(part(q), wide - 8 * q, 1)
        for step in (4, 2, 1):
            total = total + pltpu.roll(pltpu.roll(total, wide - step, 1), 8 - step, 0)
        for k in range(8):
            lags[half, 8 * n + k] = total[0:1, 128 * k : 128 * k + 128]
        return carry

    lax.fori_loop(0, SEQ * BLOCK // 1024, chunk, 0)


def kernel(
    grad_hbm, query_hbm, key_hbm, value_hbm, filter_hbm,
    out_hbm, lag_out,
    grad, query, key, value, taps_in, out,
    mixed_rows, gated_rows, turned, taps_turned,
    taps_send, taps_recv, taps,
    send, recv, strip, mixed, gated, conv, back, flipped, outer,
    back_send, back_recv, lags, lag_recv,
    load_sem, store_sem, own_sem,
    taps_ssem, taps_rsem, send_sem, recv_sem, back_ssem, back_rsem, lag_ssem, lag_rsem,
):
    seq = lax.axis_index("seq")
    ch = lax.axis_index("ch")
    me = seq * CH + ch

    loads = [
        pltpu.make_async_copy(src, dst, load_sem.at[k])
        for k, (src, dst) in enumerate(
            ((key_hbm, key), (value_hbm, value), (grad_hbm, grad), (query_hbm, query), (filter_hbm, taps_in))
        )
    ]
    for load in loads:
        load.start()

    def remote(src, dst, ssem, rsem, target):
        return pltpu.make_async_remote_copy(
            src_ref=src,
            dst_ref=dst,
            send_sem=ssem,
            recv_sem=rsem,
            device_id=target,
            device_id_type=pl.DeviceIdType.LOGICAL,
        )

    barrier = pltpu.get_barrier_semaphore()

    def greet(k, carry):
        pl.semaphore_signal(
            barrier, inc=1, device_id=me ^ (255 - k), device_id_type=pl.DeviceIdType.LOGICAL
        )
        return carry

    lax.fori_loop(0, DEVICES - 1, greet, 0, unroll=5)

    loads[0].wait()
    loads[1].wait()
    products(key, value, mixed_rows)
    loads[2].wait()
    loads[3].wait()
    products(grad, query, gated_rows)
    for tile in range(TILES):
        spread(mixed_rows, gated_rows, tile, turned, send)
    loads[4].wait()
    for half in range(2):
        lanes = pl.ds(pl.multiple_of(256 * half + 128 * (ch // 2), 128), 128)
        taps_turned[...] = taps_in[:, lanes].astype(F32).T
        picked = taps_turned[pl.ds(pl.multiple_of(64 * (ch % 2), 64), 64), :]
        taps_send[:, half, :] = picked.astype(BF16)

    pl.semaphore_wait(barrier, DEVICES - 1)

    pltpu.make_async_copy(taps_send.at[seq], taps_recv.at[seq], taps_rsem).start()

    def send_taps(k, carry):
        other = seq ^ (k + 1)
        remote(taps_send.at[other], taps_recv.at[seq], taps_ssem, taps_rsem, other * CH + ch).start()
        return carry

    lax.fori_loop(0, SEQ - 1, send_taps, 0, unroll=3)

    def exchange(src, dst, ssem, rsem):
        pltpu.make_async_copy(src.at[ch, seq], dst.at[ch, seq], rsem).start()

        def step(k, carry):
            other_seq = seq ^ ((k + 1) // CH)
            other_ch = ch ^ ((k + 1) % CH)
            target = other_seq * CH + other_ch
            remote(src.at[other_ch, other_seq], dst.at[ch, seq], ssem, rsem, target).start()
            return carry

        lax.fori_loop(0, DEVICES - 1, step, 0, unroll=5)

    for half in range(2):
        exchange(send.at[half], recv.at[half], send_sem.at[half], recv_sem.at[half])

    pltpu.make_async_copy(taps_recv, taps_recv, taps_rsem).wait()
    for half in range(2):
        taps[half] = taps_recv[:, half, :].astype(F32)
        toeplitz(taps, half, strip)

    for half in range(2):
        pltpu.make_async_copy(recv.at[half], recv.at[half], recv_sem.at[half]).wait()
        unpack(recv, half, mixed, gated)
        convolve(strip, half, mixed, gated, conv, back)
        pack(conv, back, half, back_send)
        exchange(back_send.at[half], back_recv.at[half], back_ssem.at[half], back_rsem.at[half])
        lag(mixed, gated, half, flipped, outer, lags)
        lag_ch = 2 * half + ch // 2
        lag_slot = lag_recv.at[ch % 2, seq]

        @pl.when(lag_ch == ch)
        def _():
            pltpu.make_async_copy(lags.at[half, seq], lag_slot, lag_rsem).start()

        @pl.when(lag_ch != ch)
        def _():
            remote(lags.at[half, seq], lag_slot, lag_ssem, lag_rsem, seq * CH + lag_ch).start()

        def send_lags(k, carry):
            other = seq ^ (k + 1)
            remote(lags.at[half, other], lag_slot, lag_ssem, lag_rsem, other * CH + lag_ch).start()
            return carry

        lax.fori_loop(0, SEQ - 1, send_lags, 0, unroll=3)

    stores = []
    for half in range(2):
        pltpu.make_async_copy(back_recv.at[half], back_recv.at[half], back_rsem.at[half]).wait()
        for tile in (2 * half, 2 * half + 1):
            collect(back_recv, tile, turned, mixed_rows, gated_rows)
            gradients(tile, mixed_rows, gated_rows, grad, key, value, out)
            lanes = pl.ds(128 * tile, 128)
            store = pltpu.make_async_copy(
                out.at[:, :, :, lanes], out_hbm.at[:, :, :, lanes], store_sem.at[tile]
            )
            store.start()
            stores.append(store)

    pltpu.make_async_copy(lag_recv, lag_recv, lag_rsem).wait()
    lag_out[...] = lag_recv[...].reshape(128, BLOCK).T * SCALE

    pltpu.make_async_copy(
        taps_send.at[pl.ds(0, SEQ - 1)], taps_send.at[pl.ds(0, SEQ - 1)], taps_ssem
    ).wait()
    for half in range(2):
        for buffer, sem in ((send, send_sem), (back_send, back_ssem)):
            for c in range(CH):
                piece = buffer.at[half, c, pl.ds(0, SEQ if c else SEQ - 1)]
                pltpu.make_async_copy(piece, piece, sem.at[half]).wait()

        sent = lags.at[half, pl.ds(0, SEQ - 1)]
        pltpu.make_async_copy(sent, sent, lag_ssem).wait()

        @pl.when(2 * half + ch // 2 != ch)
        def _():
            pltpu.make_async_copy(lags.at[half, 0], lags.at[half, 0], lag_ssem).wait()

    for store in stores:
        store.wait()


def local(grad_output, query_act, key_act, value_act, long_filter):
    vmem = pltpu.VMEM
    dma = pltpu.SemaphoreType.DMA
    message = (2, CH, SEQ, 8, BLOCK)
    return pl.pallas_call(
        kernel,
        out_shape=(
            jax.ShapeDtypeStruct((3, BLOCK, OWN, GROUPS), BF16),
            jax.ShapeDtypeStruct((BLOCK, 128), F32),
        ),
        in_specs=[pl.BlockSpec(memory_space=pl.ANY)] * 5,
        out_specs=[pl.BlockSpec(memory_space=pl.ANY), pl.BlockSpec(memory_space=pltpu.VMEM)],
        scratch_shapes=[
            vmem((BLOCK, OWN, GROUPS), BF16),
            vmem((BLOCK, OWN, GROUPS), BF16),
            vmem((BLOCK, OWN, GROUPS), BF16),
            vmem((BLOCK, OWN, GROUPS), BF16),
            vmem((BLOCK, GROUPS), BF16),
            vmem((3, BLOCK, OWN, GROUPS), BF16),
            vmem((TILES, BLOCK * OWN, 128), F32),
            vmem((TILES, BLOCK * OWN, 128), F32),
            vmem((1024, BLOCK), F32),
            vmem((128, BLOCK), F32),
            vmem((SEQ, 2, BLOCK), BF16),
            vmem((SEQ, 2, BLOCK), BF16),
            vmem((2, SEQ, BLOCK), F32),
            vmem(message, BF16),
            vmem(message, BF16),
            vmem((2, 128, SEQ * BLOCK + 128), BF16),
            vmem((ROWS, PAIR), BF16),
            vmem((2 * ROWS, PAIR), BF16),
            vmem((ROWS, PAIR), F32),
            vmem((ROWS, PAIR), F32),
            vmem((PAIR, ROWS), BF16),
            vmem((PAIR, SEQ * BLOCK + 256), F32),
            vmem(message, BF16),
            vmem(message, BF16),
            vmem((2, SEQ, 1, BLOCK), F32),
            vmem((2, SEQ, 1, BLOCK), F32),
            dma((5,)),
            dma((TILES,)),
            dma,
            dma,
            dma,
            dma((2,)),
            dma((2,)),
            dma((2,)),
            dma((2,)),
            dma,
            dma,
        ],
        compiler_params=pltpu.CompilerParams(
            collective_id=0, has_side_effects=True, vmem_limit_bytes=56 * 2**20
        ),
        cost_estimate=pl.CostEstimate(
            flops=10_000_000_000, bytes_accessed=4_000_000, transcendentals=0
        ),
    )(grad_output, query_act, key_act, value_act, long_filter)


def solution(mesh):
    wide = P("seq", "ch", None)
    in_specs = (wide, wide, wide, wide, P("seq", None))
    out_specs = (P(None, "seq", "ch", None), P("seq", "ch"))
    return jax.shard_map(local, mesh=mesh, in_specs=in_specs, out_specs=out_specs, check_vma=False)
```

```python
import math

import jax
import jax.numpy as jnp
from jax import lax
from jax.experimental import pallas as pl
from jax.experimental.pallas import tpu as pltpu
from jax.sharding import PartitionSpec as P

F32 = jnp.float32
BF16 = jnp.bfloat16

SEQ = 64
CH = 4
DEVICES = SEQ * CH
BLOCK = 128
MEMBERS = 16
OWN = 4
GROUPS = 512
TILES = GROUPS // 128
PAIR = 2 * BLOCK
STEPS = SEQ // 2
ROWS = STEPS * MEMBERS
SCALE = 1.0 / math.sqrt(MEMBERS * SEQ * BLOCK)


def dot_rows(left, right):
    return lax.dot_general(
        left, right, (((1,), (1,)), ((), ())), preferred_element_type=F32
    )


def dot(left, right):
    return jnp.dot(left, right, preferred_element_type=F32)


def products(left, right, rows, beside):
    def body(k, carry):
        beside(k)
        at = pl.ds(pl.multiple_of(16 * k, 16), 16)
        value = (left[at].astype(F32) * right[at].astype(F32)).astype(BF16).astype(F32)
        value = value.reshape(64, GROUPS)
        for tile in range(TILES):
            rows[tile, pl.ds(pl.multiple_of(64 * k, 64), 64), :] = value[
                :, 128 * tile : 128 * tile + 128
            ]
        return carry

    lax.fori_loop(0, BLOCK // 16, body, 0)


def spread(mixed_rows, gated_rows, tile, turned, send):
    for arr, rows in enumerate((mixed_rows, gated_rows)):
        for m in range(OWN):
            part = rows.at[tile][pl.ds(m, BLOCK, stride=OWN), :]
            turned[pl.ds(arr * OWN + m, 128, stride=8), :] = part.T
    low = 2 * (tile % 2)
    send[tile // 2, low : low + 2] = turned[...].reshape(2, SEQ, 8, BLOCK).astype(BF16)


def collect(recv, tile, turned, conv_rows, back_rows):
    low = 2 * (tile % 2)
    turned[...] = recv[tile // 2, low : low + 2].astype(F32).reshape(1024, BLOCK)
    for arr, rows in enumerate((conv_rows, back_rows)):
        for m in range(OWN):
            part = turned[pl.ds(arr * OWN + m, 128, stride=8), :]
            rows.at[tile][pl.ds(m, BLOCK, stride=OWN), :] = part.T


def gradients(tile, conv_rows, back_rows, grad, key, value, out):
    lanes = pl.ds(128 * tile, 128)

    def body(k, carry):
        at = pl.ds(pl.multiple_of(16 * k, 16), 16)
        rows = pl.ds(pl.multiple_of(64 * k, 64), 64)
        conv = conv_rows[tile, rows, :].reshape(16, OWN, 128)
        back = back_rows[tile, rows, :].reshape(16, OWN, 128)
        out[0, at, :, lanes] = (grad[at, :, lanes].astype(F32) * conv).astype(BF16)
        out[1, at, :, lanes] = (back * value[at, :, lanes].astype(F32)).astype(BF16)
        out[2, at, :, lanes] = (back * key[at, :, lanes].astype(F32)).astype(BF16)
        return carry

    lax.fori_loop(0, BLOCK // 16, body, 0)


def toeplitz(taps, half, strip):
    strip[half, :, 0:128] = jnp.zeros((128, 128), BF16)

    def body(t, carry):
        now = taps[half, pl.ds(t, 1), :]
        before = taps[half, pl.ds(jnp.maximum(t - 1, 0), 1), :] * jnp.where(t > 0, 1.0, 0.0)
        both = jnp.broadcast_to(jnp.concatenate([before, now], axis=1), (128, 256))
        skewed = pltpu.roll(both, 0, 1, stride=1, stride_axis=0)
        at = pl.ds(pl.multiple_of(128 * (t + 1), 128), 128)
        strip[half, :, at] = skewed[:, 128:].astype(BF16)
        return carry

    lax.fori_loop(0, SEQ, body, 0, unroll=8)


def unpack(recv, half, mixed, gated):
    def body(j, carry):
        rows = pl.ds(pl.multiple_of(MEMBERS * j, MEMBERS), MEMBERS)
        for h in range(2):
            inputs, gates = [], []
            for c in (0, 2):
                low = recv[half, c, 2 * j + h].astype(F32)
                high = recv[half, c + 1, 2 * j + h].astype(F32)
                inputs.append(jnp.concatenate([low[:OWN], high[:OWN]], axis=0))
                gates.append(jnp.concatenate([low[OWN:], high[OWN:]], axis=0))
            lanes = slice(128 * h, 128 * h + 128)
            mixed[rows, lanes] = jnp.concatenate(inputs, axis=0).astype(BF16)
            gated[rows, lanes] = jnp.concatenate(gates, axis=0).astype(BF16)
        return carry

    lax.fori_loop(0, STEPS, body, 0, unroll=4)


def pack(conv, back, half, send):
    def body(i, carry):
        for h in range(2):
            lanes = slice(128 * h, 128 * h + 128)
            for c in (0, 2):
                rows = pl.ds(pl.multiple_of(MEMBERS * i + OWN * c, 8), 8)
                y = conv[rows, lanes]
                m = back[rows, lanes]
                send[half, c, 2 * i + h] = jnp.concatenate([y[:OWN], m[:OWN]], axis=0).astype(BF16)
                send[half, c + 1, 2 * i + h] = jnp.concatenate([y[OWN:], m[OWN:]], axis=0).astype(BF16)
        return carry

    lax.fori_loop(0, STEPS, body, 0, unroll=4)


def convolve(strip, half, mixed, gated, conv, back):
    for d in range(STEPS):
        o = PAIR * d
        weights = jnp.concatenate(
            [strip[half, :, o + 128 : o + 384], strip[half, :, o : o + 256]], axis=0
        )
        skip = MEMBERS * d
        y = dot(mixed[0 : ROWS - skip, :], weights)
        m = dot_rows(gated[skip:ROWS, :], weights)
        if d == 0:
            conv[...] = y
            back[...] = m
        else:
            conv[skip:ROWS, :] += y
            back[0 : ROWS - skip, :] += m


def lag(mixed, gated, half, flipped, outer, lags):
    row = lax.broadcasted_iota(jnp.int32, (PAIR, PAIR), 0)
    column = lax.broadcasted_iota(jnp.int32, (PAIR, PAIR), 1)
    eye = jnp.where(row == column, 1.0, 0.0).astype(BF16)
    flipped[...] = dot_rows(eye, mixed[...]).astype(BF16)
    outer[:, SEQ * BLOCK :] = jnp.zeros((PAIR, 256), F32)
    gated[ROWS:, :] = jnp.zeros((ROWS, PAIR), BF16)
    for d in range(STEPS):
        depth = ROWS if d < STEPS // 2 else ROWS // 2
        skip = MEMBERS * d
        outer[:, PAIR * d : PAIR * d + PAIR] = dot(
            flipped[:, :depth], gated[skip : skip + depth, :]
        )
    wide = 1024 + 128

    def chunk(n, carry):
        base = pl.multiple_of(1024 * n, 128)
        after = pl.multiple_of(base + 128, 128)

        def part(q):
            first = outer[8 * q : 8 * q + 8, pl.ds(base, wide)]
            return first + outer[128 + 8 * q : 136 + 8 * q, pl.ds(after, wide)]

        total = part(0)
        for q in range(1, 16):
            total = total + pltpu.roll(part(q), wide - 8 * q, 1)
        for step in (4, 2, 1):
            total = total + pltpu.roll(pltpu.roll(total, wide - step, 1), 8 - step, 0)
        for k in range(8):
            lags[half, 8 * n + k] = total[0:1, 128 * k : 128 * k + 128]
        return carry

    lax.fori_loop(0, SEQ * BLOCK // 1024, chunk, 0)


def partner(k, seq, ch):
    turn = (k >> 3) & 7
    z = ((seq >> 1) + ((turn + 1) >> 1) * (2 * (turn & 1) - 1)) & 7
    x = ((seq >> 4) + (k >> 6)) & 3
    return (x << 4) | (z << 1) | ((seq ^ (k >> 2)) & 1), ch ^ (k & 3)


def kernel(
    grad_hbm, query_hbm, key_hbm, value_hbm, filter_hbm,
    out, lag_out,
    grad, query, key, value, taps_in,
    mixed_rows, gated_rows, turned, taps_turned,
    taps_send, taps_recv, taps,
    send, recv, strip, mixed, gated, conv, back, flipped, outer,
    back_send, back_recv, lags, lag_recv,
    load_sem,
    taps_ssem, taps_rsem, send_sem, recv_sem, back_ssem, back_rsem, lag_ssem, lag_rsem,
):
    seq = lax.axis_index("seq")
    ch = lax.axis_index("ch")
    me = seq * CH + ch

    loads = [
        pltpu.make_async_copy(src, dst, load_sem.at[k])
        for k, (src, dst) in enumerate(
            ((key_hbm, key), (value_hbm, value), (grad_hbm, grad), (query_hbm, query), (filter_hbm, taps_in))
        )
    ]
    for load in loads:
        load.start()

    def remote(src, dst, ssem, rsem, target):
        return pltpu.make_async_remote_copy(
            src_ref=src,
            dst_ref=dst,
            send_sem=ssem,
            recv_sem=rsem,
            device_id=target,
            device_id_type=pl.DeviceIdType.LOGICAL,
        )

    barrier = pltpu.get_barrier_semaphore()

    def greet(first, count):
        def signal(n):
            pl.semaphore_signal(
                barrier,
                inc=1,
                device_id=me ^ (first - n),
                device_id_type=pl.DeviceIdType.LOGICAL,
            )

        if isinstance(first, int):

            def body(n, carry):
                signal(n)
                return carry

            lax.fori_loop(0, count, body, 0, unroll=5)
        else:
            for n in range(count):
                signal(n)

    greet(255, 255)
    loads[0].wait()
    loads[1].wait()
    products(key, value, mixed_rows, lambda k: None)
    loads[2].wait()
    loads[3].wait()
    products(grad, query, gated_rows, lambda k: None)
    loads[4].wait()
    for half in range(2):
        lanes = pl.ds(pl.multiple_of(256 * half + 128 * (ch // 2), 128), 128)
        taps_turned[...] = taps_in[:, lanes].astype(F32).T
        picked = taps_turned[pl.ds(pl.multiple_of(64 * (ch % 2), 64), 64), :]
        taps_send[:, half, :] = picked.astype(BF16)
    for tile in (0, 1):
        spread(mixed_rows, gated_rows, tile, turned, send)

    pl.semaphore_wait(barrier, DEVICES - 1)

    pltpu.make_async_copy(taps_send.at[seq], taps_recv.at[seq], taps_rsem).start()

    def send_taps(k, carry):
        other = seq ^ (k + 1)
        remote(taps_send.at[other], taps_recv.at[seq], taps_ssem, taps_rsem, other * CH + ch).start()
        return carry

    lax.fori_loop(0, SEQ - 1, send_taps, 0, unroll=3)

    def exchange(src, dst, ssem, rsem):
        pltpu.make_async_copy(src.at[ch, seq], dst.at[ch, seq], rsem).start()

        def step(k, carry):
            other_seq, other_ch = partner(k + 1, seq, ch)
            target = other_seq * CH + other_ch
            remote(src.at[other_ch, other_seq], dst.at[ch, seq], ssem, rsem, target).start()
            return carry

        lax.fori_loop(0, DEVICES - 1, step, 0, unroll=5)

    exchange(send.at[0], recv.at[0], send_sem.at[0], recv_sem.at[0])
    for tile in (2, 3):
        spread(mixed_rows, gated_rows, tile, turned, send)
    exchange(send.at[1], recv.at[1], send_sem.at[1], recv_sem.at[1])

    pltpu.make_async_copy(taps_recv, taps_recv, taps_rsem).wait()
    for half in range(2):
        taps[half] = taps_recv[:, half, :].astype(F32)
        toeplitz(taps, half, strip)

    for half in range(2):
        pltpu.make_async_copy(recv.at[half], recv.at[half], recv_sem.at[half]).wait()
        unpack(recv, half, mixed, gated)
        convolve(strip, half, mixed, gated, conv, back)
        pack(conv, back, half, back_send)
        exchange(back_send.at[half], back_recv.at[half], back_ssem.at[half], back_rsem.at[half])
        lag(mixed, gated, half, flipped, outer, lags)
        lag_ch = 2 * half + ch // 2
        lag_slot = lag_recv.at[ch % 2, seq]

        @pl.when(lag_ch == ch)
        def _():
            pltpu.make_async_copy(lags.at[half, seq], lag_slot, lag_rsem).start()

        @pl.when(lag_ch != ch)
        def _():
            remote(lags.at[half, seq], lag_slot, lag_ssem, lag_rsem, seq * CH + lag_ch).start()

        def send_lags(k, carry):
            other = seq ^ (k + 1)
            remote(lags.at[half, other], lag_slot, lag_ssem, lag_rsem, other * CH + lag_ch).start()
            return carry

        lax.fori_loop(0, SEQ - 1, send_lags, 0, unroll=3)

    for half in range(2):
        pltpu.make_async_copy(back_recv.at[half], back_recv.at[half], back_rsem.at[half]).wait()
        for tile in (2 * half, 2 * half + 1):
            collect(back_recv, tile, turned, mixed_rows, gated_rows)
            gradients(tile, mixed_rows, gated_rows, grad, key, value, out)

    pltpu.make_async_copy(lag_recv, lag_recv, lag_rsem).wait()
    lag_out[...] = lag_recv[...].reshape(128, BLOCK).T * SCALE

    pltpu.make_async_copy(
        taps_send.at[pl.ds(0, SEQ - 1)], taps_send.at[pl.ds(0, SEQ - 1)], taps_ssem
    ).wait()
    for half in range(2):
        for buffer, sem in ((send, send_sem), (back_send, back_ssem)):
            for c in range(CH):
                piece = buffer.at[half, c, pl.ds(0, SEQ if c else SEQ - 1)]
                pltpu.make_async_copy(piece, piece, sem.at[half]).wait()

        sent = lags.at[half, pl.ds(0, SEQ - 1)]
        pltpu.make_async_copy(sent, sent, lag_ssem).wait()

        @pl.when(2 * half + ch // 2 != ch)
        def _():
            pltpu.make_async_copy(lags.at[half, 0], lags.at[half, 0], lag_ssem).wait()


def hand_over(out, lags, out_final, lag_final, sem):
    copies = [
        pltpu.make_async_copy(out.at[k, pl.ds(64 * h, 64)], out_final.at[k, pl.ds(64 * h, 64)], sem.at[2 * k + h])
        for k in range(3)
        for h in range(2)
    ]
    copies.append(pltpu.make_async_copy(lags, lag_final, sem.at[6]))
    for copy in copies:
        copy.start()
    for copy in copies:
        copy.wait()


def local(grad_output, query_act, key_act, value_act, long_filter):
    vmem = pltpu.VMEM
    dma = pltpu.SemaphoreType.DMA
    message = (2, CH, SEQ, 8, BLOCK)
    out, lags = pl.pallas_call(
        kernel,
        out_shape=(
            pltpu.VMEM((3, BLOCK, OWN, GROUPS), BF16),
            pltpu.VMEM((BLOCK, 128), F32),
        ),
        in_specs=[pl.BlockSpec(memory_space=pltpu.HBM)] * 5,
        out_specs=[pl.BlockSpec(memory_space=pltpu.VMEM)] * 2,
        scratch_shapes=[
            vmem((BLOCK, OWN, GROUPS), BF16),
            vmem((BLOCK, OWN, GROUPS), BF16),
            vmem((BLOCK, OWN, GROUPS), BF16),
            vmem((BLOCK, OWN, GROUPS), BF16),
            vmem((BLOCK, GROUPS), BF16),
            vmem((TILES, BLOCK * OWN, 128), F32),
            vmem((TILES, BLOCK * OWN, 128), F32),
            vmem((1024, BLOCK), F32),
            vmem((128, BLOCK), F32),
            vmem((SEQ, 2, BLOCK), BF16),
            vmem((SEQ, 2, BLOCK), BF16),
            vmem((2, SEQ, BLOCK), F32),
            vmem(message, BF16),
            vmem(message, BF16),
            vmem((2, 128, SEQ * BLOCK + 128), BF16),
            vmem((ROWS, PAIR), BF16),
            vmem((2 * ROWS, PAIR), BF16),
            vmem((ROWS, PAIR), F32),
            vmem((ROWS, PAIR), F32),
            vmem((PAIR, ROWS), BF16),
            vmem((PAIR, SEQ * BLOCK + 256), F32),
            vmem(message, BF16),
            vmem(message, BF16),
            vmem((2, SEQ, 1, BLOCK), F32),
            vmem((2, SEQ, 1, BLOCK), F32),
            dma((5,)),
            dma,
            dma,
            dma((2,)),
            dma((2,)),
            dma((2,)),
            dma((2,)),
            dma,
            dma,
        ],
        compiler_params=pltpu.CompilerParams(
            collective_id=0, has_side_effects=True, vmem_limit_bytes=56 * 2**20
        ),
        cost_estimate=pl.CostEstimate(
            flops=10_000_000_000, bytes_accessed=4_000_000, transcendentals=0
        ),
    )(grad_output, query_act, key_act, value_act, long_filter)
    return out, lags


def solution(mesh):
    wide = P("seq", "ch", None)
    in_specs = (wide, wide, wide, wide, P("seq", None))
    out_specs = (P(None, "seq", "ch", None), P("seq", "ch"))
    return jax.shard_map(local, mesh=mesh, in_specs=in_specs, out_specs=out_specs, check_vma=False)
```

```python
import math

import jax
import jax.numpy as jnp
from jax import lax
from jax.experimental import pallas as pl
from jax.experimental.pallas import tpu as pltpu
from jax.sharding import PartitionSpec as P

F32 = jnp.float32
BF16 = jnp.bfloat16

SEQ = 64
CH = 4
DEVICES = SEQ * CH
BLOCK = 128
MEMBERS = 16
OWN = 4
GROUPS = 512
TILES = GROUPS // 128
PAIR = 2 * BLOCK
STEPS = SEQ // 2
ROWS = STEPS * MEMBERS
SCALE = 1.0 / math.sqrt(MEMBERS * SEQ * BLOCK)


def dot_rows(left, right):
    return lax.dot_general(
        left, right, (((1,), (1,)), ((), ())), preferred_element_type=F32
    )


def dot(left, right):
    return jnp.dot(left, right, preferred_element_type=F32)


def products(left, right, rows, beside):
    def body(k, carry):
        beside(k)
        at = pl.ds(pl.multiple_of(16 * k, 16), 16)
        value = (left[at].astype(F32) * right[at].astype(F32)).astype(BF16).astype(F32)
        value = value.reshape(64, GROUPS)
        for tile in range(TILES):
            rows[tile, pl.ds(pl.multiple_of(64 * k, 64), 64), :] = value[
                :, 128 * tile : 128 * tile + 128
            ]
        return carry

    lax.fori_loop(0, BLOCK // 16, body, 0)


def spread(mixed_rows, gated_rows, tile, turned, send):
    for arr, rows in enumerate((mixed_rows, gated_rows)):
        for m in range(OWN):
            part = rows.at[tile][pl.ds(m, BLOCK, stride=OWN), :]
            turned[pl.ds(arr * OWN + m, 128, stride=8), :] = part.T
    low = 2 * (tile % 2)
    send[tile // 2, low : low + 2] = turned[...].reshape(2, SEQ, 8, BLOCK).astype(BF16)


def collect(recv, tile, turned, conv_rows, back_rows):
    low = 2 * (tile % 2)
    turned[...] = recv[tile // 2, low : low + 2].astype(F32).reshape(1024, BLOCK)
    for arr, rows in enumerate((conv_rows, back_rows)):
        for m in range(OWN):
            part = turned[pl.ds(arr * OWN + m, 128, stride=8), :]
            rows.at[tile][pl.ds(m, BLOCK, stride=OWN), :] = part.T


def gradients(tile, conv_rows, back_rows, grad, key, value, out):
    lanes = pl.ds(128 * tile, 128)

    def body(k, carry):
        at = pl.ds(pl.multiple_of(16 * k, 16), 16)
        rows = pl.ds(pl.multiple_of(64 * k, 64), 64)
        conv = conv_rows[tile, rows, :].reshape(16, OWN, 128)
        back = back_rows[tile, rows, :].reshape(16, OWN, 128)
        out[0, at, :, lanes] = (grad[at, :, lanes].astype(F32) * conv).astype(BF16)
        out[1, at, :, lanes] = (back * value[at, :, lanes].astype(F32)).astype(BF16)
        out[2, at, :, lanes] = (back * key[at, :, lanes].astype(F32)).astype(BF16)
        return carry

    lax.fori_loop(0, BLOCK // 16, body, 0)


def toeplitz(taps, half, strip):
    strip[half, :, 0:128] = jnp.zeros((128, 128), BF16)

    def body(t, carry):
        now = taps[half, pl.ds(t, 1), :]
        before = taps[half, pl.ds(jnp.maximum(t - 1, 0), 1), :] * jnp.where(t > 0, 1.0, 0.0)
        both = jnp.broadcast_to(jnp.concatenate([before, now], axis=1), (128, 256))
        skewed = pltpu.roll(both, 0, 1, stride=1, stride_axis=0)
        at = pl.ds(pl.multiple_of(128 * (t + 1), 128), 128)
        strip[half, :, at] = skewed[:, 128:].astype(BF16)
        return carry

    lax.fori_loop(0, SEQ, body, 0, unroll=8)


def unpack(recv, half, mixed, gated):
    def body(j, carry):
        rows = pl.ds(pl.multiple_of(MEMBERS * j, MEMBERS), MEMBERS)
        for h in range(2):
            inputs, gates = [], []
            for c in (0, 2):
                low = recv[half, c, 2 * j + h].astype(F32)
                high = recv[half, c + 1, 2 * j + h].astype(F32)
                inputs.append(jnp.concatenate([low[:OWN], high[:OWN]], axis=0))
                gates.append(jnp.concatenate([low[OWN:], high[OWN:]], axis=0))
            lanes = slice(128 * h, 128 * h + 128)
            mixed[rows, lanes] = jnp.concatenate(inputs, axis=0).astype(BF16)
            gated[rows, lanes] = jnp.concatenate(gates, axis=0).astype(BF16)
        return carry

    lax.fori_loop(0, STEPS, body, 0, unroll=4)


def pack(conv, back, half, send):
    def body(i, carry):
        for h in range(2):
            lanes = slice(128 * h, 128 * h + 128)
            for c in (0, 2):
                rows = pl.ds(pl.multiple_of(MEMBERS * i + OWN * c, 8), 8)
                y = conv[rows, lanes]
                m = back[rows, lanes]
                send[half, c, 2 * i + h] = jnp.concatenate([y[:OWN], m[:OWN]], axis=0).astype(BF16)
                send[half, c + 1, 2 * i + h] = jnp.concatenate([y[OWN:], m[OWN:]], axis=0).astype(BF16)
        return carry

    lax.fori_loop(0, STEPS, body, 0, unroll=4)


def convolve(strip, half, mixed, gated, conv, back):
    for d in range(STEPS):
        o = PAIR * d
        weights = jnp.concatenate(
            [strip[half, :, o + 128 : o + 384], strip[half, :, o : o + 256]], axis=0
        )
        skip = MEMBERS * d
        y = dot(mixed[0 : ROWS - skip, :], weights)
        m = dot_rows(gated[skip:ROWS, :], weights)
        if d == 0:
            conv[...] = y
            back[...] = m
        else:
            conv[skip:ROWS, :] += y
            back[0 : ROWS - skip, :] += m


def lag(mixed, gated, half, flipped, outer, lags):
    row = lax.broadcasted_iota(jnp.int32, (PAIR, PAIR), 0)
    column = lax.broadcasted_iota(jnp.int32, (PAIR, PAIR), 1)
    eye = jnp.where(row == column, 1.0, 0.0).astype(BF16)
    flipped[...] = dot_rows(eye, mixed[...]).astype(BF16)
    outer[:, SEQ * BLOCK :] = jnp.zeros((PAIR, 256), F32)
    gated[ROWS:, :] = jnp.zeros((ROWS, PAIR), BF16)
    for d in range(STEPS):
        depth = ROWS if d < STEPS // 2 else ROWS // 2
        skip = MEMBERS * d
        outer[:, PAIR * d : PAIR * d + PAIR] = dot(
            flipped[:, :depth], gated[skip : skip + depth, :]
        )
    wide = 1024 + 128

    def chunk(n, carry):
        base = pl.multiple_of(1024 * n, 128)
        after = pl.multiple_of(base + 128, 128)

        def part(q):
            first = outer[8 * q : 8 * q + 8, pl.ds(base, wide)]
            return first + outer[128 + 8 * q : 136 + 8 * q, pl.ds(after, wide)]

        total = part(0)
        for q in range(1, 16):
            total = total + pltpu.roll(part(q), wide - 8 * q, 1)
        for step in (4, 2, 1):
            total = total + pltpu.roll(pltpu.roll(total, wide - step, 1), 8 - step, 0)
        for k in range(8):
            lags[half, 8 * n + k] = total[0:1, 128 * k : 128 * k + 128]
        return carry

    lax.fori_loop(0, SEQ * BLOCK // 1024, chunk, 0)


def partner(k, seq, ch):
    k = (k + 248) & 255
    turn = 7 - ((k >> 3) & 7)
    z = ((seq >> 1) + ((turn + 1) >> 1) * (2 * (turn & 1) - 1)) & 7
    far = k >> 6
    x = ((seq >> 4) + 2 - far - (far >> 1) - 2 * ((far >> 1) & far)) & 3
    return (x << 4) | (z << 1) | ((seq ^ (k >> 2)) & 1), ch ^ (k & 3)


def kernel(
    grad_hbm, query_hbm, key_hbm, value_hbm, filter_hbm,
    out, lag_out,
    grad, query, key, value, taps_in,
    mixed_rows, gated_rows, turned, taps_turned,
    taps_send, taps_recv, taps,
    send, recv, strip, mixed, gated, conv, back, flipped, outer,
    back_send, back_recv, lags, lag_recv,
    load_sem,
    taps_ssem, taps_rsem, send_sem, recv_sem, back_ssem, back_rsem, lag_ssem, lag_rsem,
):
    seq = lax.axis_index("seq")
    ch = lax.axis_index("ch")
    me = seq * CH + ch

    loads = [
        pltpu.make_async_copy(src, dst, load_sem.at[k])
        for k, (src, dst) in enumerate(
            ((key_hbm, key), (value_hbm, value), (grad_hbm, grad), (query_hbm, query), (filter_hbm, taps_in))
        )
    ]
    for load in loads:
        load.start()

    def remote(src, dst, ssem, rsem, target):
        return pltpu.make_async_remote_copy(
            src_ref=src,
            dst_ref=dst,
            send_sem=ssem,
            recv_sem=rsem,
            device_id=target,
            device_id_type=pl.DeviceIdType.LOGICAL,
        )

    barrier = pltpu.get_barrier_semaphore()

    def greet(first, count):
        def signal(n):
            pl.semaphore_signal(
                barrier,
                inc=1,
                device_id=me ^ (first - n),
                device_id_type=pl.DeviceIdType.LOGICAL,
            )

        if isinstance(first, int):

            def body(n, carry):
                signal(n)
                return carry

            lax.fori_loop(0, count, body, 0, unroll=51)
        else:
            for n in range(count):
                signal(n)

    greet(255, 255)
    loads[0].wait()
    loads[1].wait()
    products(key, value, mixed_rows, lambda k: None)
    loads[2].wait()
    loads[3].wait()
    products(grad, query, gated_rows, lambda k: None)
    loads[4].wait()
    for half in range(2):
        lanes = pl.ds(pl.multiple_of(256 * half + 128 * (ch // 2), 128), 128)
        taps_turned[...] = taps_in[:, lanes].astype(F32).T
        picked = taps_turned[pl.ds(pl.multiple_of(64 * (ch % 2), 64), 64), :]
        taps_send[:, half, :] = picked.astype(BF16)
    for tile in (0, 1):
        spread(mixed_rows, gated_rows, tile, turned, send)

    pl.semaphore_wait(barrier, DEVICES - 1)

    pltpu.make_async_copy(taps_send.at[seq], taps_recv.at[seq], taps_rsem).start()

    def send_taps(k, carry):
        other = seq ^ (k + 1)
        remote(taps_send.at[other], taps_recv.at[seq], taps_ssem, taps_rsem, other * CH + ch).start()
        return carry

    lax.fori_loop(0, SEQ - 1, send_taps, 0, unroll=3)

    def exchange(src, dst, ssem, rsem):
        pltpu.make_async_copy(src.at[ch, seq], dst.at[ch, seq], rsem).start()

        def step(k, carry):
            other_seq, other_ch = partner(k + 1, seq, ch)
            target = other_seq * CH + other_ch
            remote(src.at[other_ch, other_seq], dst.at[ch, seq], ssem, rsem, target).start()
            return carry

        lax.fori_loop(0, DEVICES - 1, step, 0, unroll=17)

    exchange(send.at[0], recv.at[0], send_sem.at[0], recv_sem.at[0])
    for tile in (2, 3):
        spread(mixed_rows, gated_rows, tile, turned, send)
    exchange(send.at[1], recv.at[1], send_sem.at[1], recv_sem.at[1])

    pltpu.make_async_copy(taps_recv, taps_recv, taps_rsem).wait()
    for half in range(2):
        taps[half] = taps_recv[:, half, :].astype(F32)
        toeplitz(taps, half, strip)

    for half in range(2):
        pltpu.make_async_copy(recv.at[half], recv.at[half], recv_sem.at[half]).wait()
        unpack(recv, half, mixed, gated)
        convolve(strip, half, mixed, gated, conv, back)
        pack(conv, back, half, back_send)
        exchange(back_send.at[half], back_recv.at[half], back_ssem.at[half], back_rsem.at[half])
        lag(mixed, gated, half, flipped, outer, lags)
        lag_ch = 2 * half + ch // 2
        lag_slot = lag_recv.at[ch % 2, seq]

        @pl.when(lag_ch == ch)
        def _():
            pltpu.make_async_copy(lags.at[half, seq], lag_slot, lag_rsem).start()

        @pl.when(lag_ch != ch)
        def _():
            remote(lags.at[half, seq], lag_slot, lag_ssem, lag_rsem, seq * CH + lag_ch).start()

        def send_lags(k, carry):
            other = seq ^ (k + 1)
            remote(lags.at[half, other], lag_slot, lag_ssem, lag_rsem, other * CH + lag_ch).start()
            return carry

        lax.fori_loop(0, SEQ - 1, send_lags, 0, unroll=3)

    for half in range(2):
        pltpu.make_async_copy(back_recv.at[half], back_recv.at[half], back_rsem.at[half]).wait()
        for tile in (2 * half, 2 * half + 1):
            collect(back_recv, tile, turned, mixed_rows, gated_rows)
            gradients(tile, mixed_rows, gated_rows, grad, key, value, out)

    pltpu.make_async_copy(lag_recv, lag_recv, lag_rsem).wait()
    lag_out[...] = lag_recv[...].reshape(128, BLOCK).T * SCALE

    pltpu.make_async_copy(
        taps_send.at[pl.ds(0, SEQ - 1)], taps_send.at[pl.ds(0, SEQ - 1)], taps_ssem
    ).wait()
    for half in range(2):
        for buffer, sem in ((send, send_sem), (back_send, back_ssem)):
            for c in range(CH):
                piece = buffer.at[half, c, pl.ds(0, SEQ if c else SEQ - 1)]
                pltpu.make_async_copy(piece, piece, sem.at[half]).wait()

        sent = lags.at[half, pl.ds(0, SEQ - 1)]
        pltpu.make_async_copy(sent, sent, lag_ssem).wait()

        @pl.when(2 * half + ch // 2 != ch)
        def _():
            pltpu.make_async_copy(lags.at[half, 0], lags.at[half, 0], lag_ssem).wait()


def hand_over(out, lags, out_final, lag_final, sem):
    copies = [
        pltpu.make_async_copy(out.at[k, pl.ds(64 * h, 64)], out_final.at[k, pl.ds(64 * h, 64)], sem.at[2 * k + h])
        for k in range(3)
        for h in range(2)
    ]
    copies.append(pltpu.make_async_copy(lags, lag_final, sem.at[6]))
    for copy in copies:
        copy.start()
    for copy in copies:
        copy.wait()


def local(grad_output, query_act, key_act, value_act, long_filter):
    vmem = pltpu.VMEM
    dma = pltpu.SemaphoreType.DMA
    message = (2, CH, SEQ, 8, BLOCK)
    out, lags = pl.pallas_call(
        kernel,
        out_shape=(
            pltpu.VMEM((3, BLOCK, OWN, GROUPS), BF16),
            pltpu.VMEM((BLOCK, 128), F32),
        ),
        in_specs=[pl.BlockSpec(memory_space=pltpu.HBM)] * 5,
        out_specs=[pl.BlockSpec(memory_space=pltpu.VMEM)] * 2,
        scratch_shapes=[
            vmem((BLOCK, OWN, GROUPS), BF16),
            vmem((BLOCK, OWN, GROUPS), BF16),
            vmem((BLOCK, OWN, GROUPS), BF16),
            vmem((BLOCK, OWN, GROUPS), BF16),
            vmem((BLOCK, GROUPS), BF16),
            vmem((TILES, BLOCK * OWN, 128), F32),
            vmem((TILES, BLOCK * OWN, 128), F32),
            vmem((1024, BLOCK), F32),
            vmem((128, BLOCK), F32),
            vmem((SEQ, 2, BLOCK), BF16),
            vmem((SEQ, 2, BLOCK), BF16),
            vmem((2, SEQ, BLOCK), F32),
            vmem(message, BF16),
            vmem(message, BF16),
            vmem((2, 128, SEQ * BLOCK + 128), BF16),
            vmem((ROWS, PAIR), BF16),
            vmem((2 * ROWS, PAIR), BF16),
            vmem((ROWS, PAIR), F32),
            vmem((ROWS, PAIR), F32),
            vmem((PAIR, ROWS), BF16),
            vmem((PAIR, SEQ * BLOCK + 256), F32),
            vmem(message, BF16),
            vmem(message, BF16),
            vmem((2, SEQ, 1, BLOCK), F32),
            vmem((2, SEQ, 1, BLOCK), F32),
            dma((5,)),
            dma,
            dma,
            dma((2,)),
            dma((2,)),
            dma((2,)),
            dma((2,)),
            dma,
            dma,
        ],
        compiler_params=pltpu.CompilerParams(
            collective_id=0, has_side_effects=True, vmem_limit_bytes=56 * 2**20
        ),
        cost_estimate=pl.CostEstimate(
            flops=10_000_000_000, bytes_accessed=4_000_000, transcendentals=0
        ),
    )(grad_output, query_act, key_act, value_act, long_filter)
    return out, lags


def solution(mesh):
    wide = P("seq", "ch", None)
    in_specs = (wide, wide, wide, wide, P("seq", None))
    out_specs = (P(None, "seq", "ch", None), P("seq", "ch"))
    return jax.shard_map(local, mesh=mesh, in_specs=in_specs, out_specs=out_specs, check_vma=False)
```

```python
import math

import jax
import jax.numpy as jnp
from jax import lax
from jax.experimental import pallas as pl
from jax.experimental.pallas import tpu as pltpu
from jax.sharding import PartitionSpec as P

F32 = jnp.float32
BF16 = jnp.bfloat16

SEQ = 64
CH = 4
DEVICES = SEQ * CH
BLOCK = 128
MEMBERS = 16
OWN = 4
GROUPS = 512
TILES = GROUPS // 128
PAIR = 2 * BLOCK
STEPS = SEQ // 2
ROWS = STEPS * MEMBERS
SCALE = 1.0 / math.sqrt(MEMBERS * SEQ * BLOCK)


def dot_rows(left, right):
    return lax.dot_general(
        left, right, (((1,), (1,)), ((), ())), preferred_element_type=F32
    )


def dot(left, right):
    return jnp.dot(left, right, preferred_element_type=F32)


def products(left, right, half, rows):
    lanes = slice(256 * half, 256 * half + 256)

    def body(k, carry):
        at = pl.ds(pl.multiple_of(16 * k, 16), 16)
        value = left[at, :, lanes].astype(F32) * right[at, :, lanes].astype(F32)
        value = value.astype(BF16).astype(F32).reshape(64, 256)
        at = pl.ds(pl.multiple_of(64 * k, 64), 64)
        rows[2 * half, at, :] = value[:, :128]
        rows[2 * half + 1, at, :] = value[:, 128:]
        return carry

    lax.fori_loop(0, BLOCK // 16, body, 0)


def spread(mixed_rows, gated_rows, tile, turned, send):
    for arr, rows in enumerate((mixed_rows, gated_rows)):
        for m in range(OWN):
            part = rows.at[tile][pl.ds(m, BLOCK, stride=OWN), :]
            turned[pl.ds(arr * OWN + m, 128, stride=8), :] = part.T
    low = 2 * (tile % 2)
    send[tile // 2, low : low + 2] = turned[...].reshape(2, SEQ, 8, BLOCK).astype(BF16)


def collect(recv, tile, turned, conv_rows, back_rows):
    low = 2 * (tile % 2)
    turned[...] = recv[tile // 2, low : low + 2].astype(F32).reshape(1024, BLOCK)
    for arr, rows in enumerate((conv_rows, back_rows)):
        for m in range(OWN):
            part = turned[pl.ds(arr * OWN + m, 128, stride=8), :]
            rows.at[tile][pl.ds(m, BLOCK, stride=OWN), :] = part.T


def gradients(tile, conv_rows, back_rows, grad, key, value, out):
    lanes = pl.ds(128 * tile, 128)

    def body(k, carry):
        at = pl.ds(pl.multiple_of(16 * k, 16), 16)
        rows = pl.ds(pl.multiple_of(64 * k, 64), 64)
        conv = conv_rows[tile, rows, :].reshape(16, OWN, 128)
        back = back_rows[tile, rows, :].reshape(16, OWN, 128)
        out[0, at, :, lanes] = (grad[at, :, lanes].astype(F32) * conv).astype(BF16)
        out[1, at, :, lanes] = (back * value[at, :, lanes].astype(F32)).astype(BF16)
        out[2, at, :, lanes] = (back * key[at, :, lanes].astype(F32)).astype(BF16)
        return carry

    lax.fori_loop(0, BLOCK // 16, body, 0)


def toeplitz(taps, half, strip):
    strip[half, :, 0:128] = jnp.zeros((128, 128), BF16)

    def body(t, carry):
        now = taps[half, pl.ds(t, 1), :]
        before = taps[half, pl.ds(jnp.maximum(t - 1, 0), 1), :] * jnp.where(t > 0, 1.0, 0.0)
        both = jnp.broadcast_to(jnp.concatenate([before, now], axis=1), (128, 256))
        skewed = pltpu.roll(both, 0, 1, stride=1, stride_axis=0)
        at = pl.ds(pl.multiple_of(128 * (t + 1), 128), 128)
        strip[half, :, at] = skewed[:, 128:].astype(BF16)
        return carry

    lax.fori_loop(0, SEQ, body, 0, unroll=8)


def unpack(recv, half, mixed, gated):
    def body(j, carry):
        rows = pl.ds(pl.multiple_of(MEMBERS * j, MEMBERS), MEMBERS)
        for h in range(2):
            inputs, gates = [], []
            for c in (0, 2):
                low = recv[half, c, 2 * j + h].astype(F32)
                high = recv[half, c + 1, 2 * j + h].astype(F32)
                inputs.append(jnp.concatenate([low[:OWN], high[:OWN]], axis=0))
                gates.append(jnp.concatenate([low[OWN:], high[OWN:]], axis=0))
            lanes = slice(128 * h, 128 * h + 128)
            mixed[rows, lanes] = jnp.concatenate(inputs, axis=0).astype(BF16)
            gated[rows, lanes] = jnp.concatenate(gates, axis=0).astype(BF16)
        return carry

    lax.fori_loop(0, STEPS, body, 0, unroll=4)


def pack(conv, back, half, send):
    def body(i, carry):
        for h in range(2):
            lanes = slice(128 * h, 128 * h + 128)
            for c in (0, 2):
                rows = pl.ds(pl.multiple_of(MEMBERS * i + OWN * c, 8), 8)
                y = conv[rows, lanes]
                m = back[rows, lanes]
                send[half, c, 2 * i + h] = jnp.concatenate([y[:OWN], m[:OWN]], axis=0).astype(BF16)
                send[half, c + 1, 2 * i + h] = jnp.concatenate([y[OWN:], m[OWN:]], axis=0).astype(BF16)
        return carry

    lax.fori_loop(0, STEPS, body, 0, unroll=4)


def convolve(strip, half, mixed, gated, conv, back):
    for d in range(STEPS):
        o = PAIR * d
        weights = jnp.concatenate(
            [strip[half, :, o + 128 : o + 384], strip[half, :, o : o + 256]], axis=0
        )
        skip = MEMBERS * d
        y = dot(mixed[0 : ROWS - skip, :], weights)
        m = dot_rows(gated[skip:ROWS, :], weights)
        if d == 0:
            conv[...] = y
            back[...] = m
        else:
            conv[skip:ROWS, :] += y
            back[0 : ROWS - skip, :] += m


def lag(mixed, gated, half, flipped, outer, lags):
    row = lax.broadcasted_iota(jnp.int32, (PAIR, PAIR), 0)
    column = lax.broadcasted_iota(jnp.int32, (PAIR, PAIR), 1)
    eye = jnp.where(row == column, 1.0, 0.0).astype(BF16)
    flipped[...] = dot_rows(eye, mixed[...]).astype(BF16)
    outer[:, SEQ * BLOCK :] = jnp.zeros((PAIR, 256), F32)
    gated[ROWS:, :] = jnp.zeros((ROWS, PAIR), BF16)
    for d in range(STEPS):
        depth = ROWS if d < STEPS // 2 else ROWS // 2
        skip = MEMBERS * d
        outer[:, PAIR * d : PAIR * d + PAIR] = dot(
            flipped[:, :depth], gated[skip : skip + depth, :]
        )
    wide = 1024 + 128

    def chunk(n, carry):
        base = pl.multiple_of(1024 * n, 128)
        after = pl.multiple_of(base + 128, 128)

        def part(q):
            first = outer[8 * q : 8 * q + 8, pl.ds(base, wide)]
            return first + outer[128 + 8 * q : 136 + 8 * q, pl.ds(after, wide)]

        total = part(0)
        for q in range(1, 16):
            total = total + pltpu.roll(part(q), wide - 8 * q, 1)
        for step in (4, 2, 1):
            total = total + pltpu.roll(pltpu.roll(total, wide - step, 1), 8 - step, 0)
        for k in range(8):
            lags[half, 8 * n + k] = total[0:1, 128 * k : 128 * k + 128]
        return carry

    lax.fori_loop(0, SEQ * BLOCK // 1024, chunk, 0, unroll=4)


def partner(k, seq, ch):
    k = (k + 248) & 255
    turn = 7 - ((k >> 3) & 7)
    z = ((seq >> 1) + ((turn + 1) >> 1) * (2 * (turn & 1) - 1)) & 7
    far = k >> 6
    x = ((seq >> 4) + 2 - far - (far >> 1) - 2 * ((far >> 1) & far)) & 3
    return (x << 4) | (z << 1) | ((seq ^ (k >> 2)) & 1), ch ^ (k & 3)


def kernel(
    grad_hbm, query_hbm, key_hbm, value_hbm, filter_hbm,
    out, lag_out,
    grad, query, key, value, taps_in,
    mixed_rows, gated_rows, turned, taps_turned,
    taps_send, taps_recv, taps,
    send, recv, strip, mixed, gated, conv, back, flipped, outer,
    back_send, back_recv, lags, lag_recv,
    load_sem,
    taps_ssem, taps_rsem, send_sem, recv_sem, back_ssem, back_rsem, lag_ssem, lag_rsem,
):
    seq = lax.axis_index("seq")
    ch = lax.axis_index("ch")
    me = seq * CH + ch

    loads = [
        pltpu.make_async_copy(src, dst, load_sem.at[k])
        for k, (src, dst) in enumerate(
            ((key_hbm, key), (value_hbm, value), (grad_hbm, grad), (query_hbm, query), (filter_hbm, taps_in))
        )
    ]
    for load in loads:
        load.start()

    def remote(src, dst, ssem, rsem, target):
        return pltpu.make_async_remote_copy(
            src_ref=src,
            dst_ref=dst,
            send_sem=ssem,
            recv_sem=rsem,
            device_id=target,
            device_id_type=pl.DeviceIdType.LOGICAL,
        )

    barrier = pltpu.get_barrier_semaphore()

    far = 0b10100111

    def greet(k, carry):
        pl.semaphore_signal(
            barrier, inc=1, device_id=me ^ far ^ k, device_id_type=pl.DeviceIdType.LOGICAL
        )
        return carry

    lax.fori_loop(0, far, greet, 0, unroll=167)
    lax.fori_loop(far + 1, DEVICES, greet, 0, unroll=44)

    loads[0].wait()
    loads[1].wait()
    products(key, value, 0, mixed_rows)
    loads[2].wait()
    loads[3].wait()
    products(grad, query, 0, gated_rows)
    loads[4].wait()
    for half in range(2):
        lanes = pl.ds(pl.multiple_of(256 * half + 128 * (ch // 2), 128), 128)
        taps_turned[...] = taps_in[:, lanes].astype(F32).T
        picked = taps_turned[pl.ds(pl.multiple_of(64 * (ch % 2), 64), 64), :]
        taps_send[:, half, :] = picked.astype(BF16)
    for tile in (0, 1):
        spread(mixed_rows, gated_rows, tile, turned, send)

    pl.semaphore_wait(barrier, DEVICES - 1)

    pltpu.make_async_copy(taps_send.at[seq], taps_recv.at[seq], taps_rsem).start()

    def send_taps(k, carry):
        other = seq ^ (k + 1)
        remote(taps_send.at[other], taps_recv.at[seq], taps_ssem, taps_rsem, other * CH + ch).start()
        return carry

    lax.fori_loop(0, SEQ - 1, send_taps, 0, unroll=21)

    def exchange(src, dst, ssem, rsem):
        pltpu.make_async_copy(src.at[ch, seq], dst.at[ch, seq], rsem).start()

        def step(k, carry):
            other_seq, other_ch = partner(k + 1, seq, ch)
            target = other_seq * CH + other_ch
            remote(src.at[other_ch, other_seq], dst.at[ch, seq], ssem, rsem, target).start()
            return carry

        lax.fori_loop(0, DEVICES - 1, step, 0, unroll=17)

    exchange(send.at[0], recv.at[0], send_sem.at[0], recv_sem.at[0])
    products(key, value, 1, mixed_rows)
    products(grad, query, 1, gated_rows)
    for tile in (2, 3):
        spread(mixed_rows, gated_rows, tile, turned, send)
    exchange(send.at[1], recv.at[1], send_sem.at[1], recv_sem.at[1])

    pltpu.make_async_copy(taps_recv, taps_recv, taps_rsem).wait()
    for half in range(2):
        taps[half] = taps_recv[:, half, :].astype(F32)
        toeplitz(taps, half, strip)

    for half in range(2):
        pltpu.make_async_copy(recv.at[half], recv.at[half], recv_sem.at[half]).wait()
        unpack(recv, half, mixed, gated)
        convolve(strip, half, mixed, gated, conv, back)
        pack(conv, back, half, back_send)
        exchange(back_send.at[half], back_recv.at[half], back_ssem.at[half], back_rsem.at[half])
        lag(mixed, gated, half, flipped, outer, lags)
        lag_ch = 2 * half + ch // 2
        lag_slot = lag_recv.at[ch % 2, seq]

        @pl.when(lag_ch == ch)
        def _():
            pltpu.make_async_copy(lags.at[half, seq], lag_slot, lag_rsem).start()

        @pl.when(lag_ch != ch)
        def _():
            remote(lags.at[half, seq], lag_slot, lag_ssem, lag_rsem, seq * CH + lag_ch).start()

        def send_lags(k, carry):
            other = seq ^ (k + 1)
            remote(lags.at[half, other], lag_slot, lag_ssem, lag_rsem, other * CH + lag_ch).start()
            return carry

        lax.fori_loop(0, SEQ - 1, send_lags, 0, unroll=21)

    for half in range(2):
        pltpu.make_async_copy(back_recv.at[half], back_recv.at[half], back_rsem.at[half]).wait()
        for tile in (2 * half, 2 * half + 1):
            collect(back_recv, tile, turned, mixed_rows, gated_rows)
            gradients(tile, mixed_rows, gated_rows, grad, key, value, out)

    pltpu.make_async_copy(lag_recv, lag_recv, lag_rsem).wait()
    lag_out[...] = lag_recv[...].reshape(128, BLOCK).T * SCALE

    pltpu.make_async_copy(
        taps_send.at[pl.ds(0, SEQ - 1)], taps_send.at[pl.ds(0, SEQ - 1)], taps_ssem
    ).wait()
    for half in range(2):
        for buffer, sem in ((send, send_sem), (back_send, back_ssem)):
            for c in range(CH):
                piece = buffer.at[half, c, pl.ds(0, SEQ if c else SEQ - 1)]
                pltpu.make_async_copy(piece, piece, sem.at[half]).wait()

        sent = lags.at[half, pl.ds(0, SEQ - 1)]
        pltpu.make_async_copy(sent, sent, lag_ssem).wait()

        @pl.when(2 * half + ch // 2 != ch)
        def _():
            pltpu.make_async_copy(lags.at[half, 0], lags.at[half, 0], lag_ssem).wait()


def hand_over(out, lags, out_final, lag_final, sem):
    copies = [
        pltpu.make_async_copy(out.at[k, pl.ds(64 * h, 64)], out_final.at[k, pl.ds(64 * h, 64)], sem.at[2 * k + h])
        for k in range(3)
        for h in range(2)
    ]
    copies.append(pltpu.make_async_copy(lags, lag_final, sem.at[6]))
    for copy in copies:
        copy.start()
    for copy in copies:
        copy.wait()


def local(grad_output, query_act, key_act, value_act, long_filter):
    vmem = pltpu.VMEM
    dma = pltpu.SemaphoreType.DMA
    message = (2, CH, SEQ, 8, BLOCK)
    out, lags = pl.pallas_call(
        kernel,
        out_shape=(
            pltpu.VMEM((3, BLOCK, OWN, GROUPS), BF16),
            pltpu.VMEM((BLOCK, 128), F32),
        ),
        in_specs=[pl.BlockSpec(memory_space=pltpu.HBM)] * 5,
        out_specs=[pl.BlockSpec(memory_space=pltpu.VMEM)] * 2,
        scratch_shapes=[
            vmem((BLOCK, OWN, GROUPS), BF16),
            vmem((BLOCK, OWN, GROUPS), BF16),
            vmem((BLOCK, OWN, GROUPS), BF16),
            vmem((BLOCK, OWN, GROUPS), BF16),
            vmem((BLOCK, GROUPS), BF16),
            vmem((TILES, BLOCK * OWN, 128), F32),
            vmem((TILES, BLOCK * OWN, 128), F32),
            vmem((1024, BLOCK), F32),
            vmem((128, BLOCK), F32),
            vmem((SEQ, 2, BLOCK), BF16),
            vmem((SEQ, 2, BLOCK), BF16),
            vmem((2, SEQ, BLOCK), F32),
            vmem(message, BF16),
            vmem(message, BF16),
            vmem((2, 128, SEQ * BLOCK + 128), BF16),
            vmem((ROWS, PAIR), BF16),
            vmem((2 * ROWS, PAIR), BF16),
            vmem((ROWS, PAIR), F32),
            vmem((ROWS, PAIR), F32),
            vmem((PAIR, ROWS), BF16),
            vmem((PAIR, SEQ * BLOCK + 256), F32),
            vmem(message, BF16),
            vmem(message, BF16),
            vmem((2, SEQ, 1, BLOCK), F32),
            vmem((2, SEQ, 1, BLOCK), F32),
            dma((5,)),
            dma,
            dma,
            dma((2,)),
            dma((2,)),
            dma((2,)),
            dma((2,)),
            dma,
            dma,
        ],
        compiler_params=pltpu.CompilerParams(
            collective_id=0, has_side_effects=True, vmem_limit_bytes=56 * 2**20
        ),
        cost_estimate=pl.CostEstimate(
            flops=10_000_000_000, bytes_accessed=4_000_000, transcendentals=0
        ),
    )(grad_output, query_act, key_act, value_act, long_filter)
    return out, lags


def solution(mesh):
    wide = P("seq", "ch", None)
    in_specs = (wide, wide, wide, wide, P("seq", None))
    out_specs = (P(None, "seq", "ch", None), P("seq", "ch"))
    return jax.shard_map(local, mesh=mesh, in_specs=in_specs, out_specs=out_specs, check_vma=False)
```

```python
import math

import jax
import jax.numpy as jnp
from jax import lax
from jax.experimental import pallas as pl
from jax.experimental.pallas import tpu as pltpu
from jax.sharding import PartitionSpec as P

F32 = jnp.float32
BF16 = jnp.bfloat16

SEQ = 64
CH = 4
DEVICES = SEQ * CH
BLOCK = 128
MEMBERS = 16
OWN = 4
GROUPS = 512
TILES = GROUPS // 128
PAIR = 2 * BLOCK
STEPS = SEQ // 2
ROWS = STEPS * MEMBERS
SCALE = 1.0 / math.sqrt(MEMBERS * SEQ * BLOCK)


def dot_rows(left, right):
    return lax.dot_general(
        left, right, (((1,), (1,)), ((), ())), preferred_element_type=F32
    )


def dot(left, right):
    return jnp.dot(left, right, preferred_element_type=F32)


def products(left, right, half, rows):
    lanes = slice(256 * half, 256 * half + 256)

    def body(k, carry):
        at = pl.ds(pl.multiple_of(16 * k, 16), 16)
        value = left[at, :, lanes].astype(F32) * right[at, :, lanes].astype(F32)
        value = value.astype(BF16).astype(F32).reshape(64, 256)
        at = pl.ds(pl.multiple_of(64 * k, 64), 64)
        rows[2 * half, at, :] = value[:, :128]
        rows[2 * half + 1, at, :] = value[:, 128:]
        return carry

    lax.fori_loop(0, BLOCK // 16, body, 0)


def spread(mixed_rows, gated_rows, tile, turned, send):
    for arr, rows in enumerate((mixed_rows, gated_rows)):
        for m in range(OWN):
            part = rows.at[tile][pl.ds(m, BLOCK, stride=OWN), :]
            turned[pl.ds(arr * OWN + m, 128, stride=8), :] = part.T
    low = 2 * (tile % 2)
    send[tile // 2, low : low + 2] = turned[...].reshape(2, SEQ, 8, BLOCK).astype(BF16)


def collect(recv, tile, turned, conv_rows, back_rows):
    low = 2 * (tile % 2)
    turned[...] = recv[tile // 2, low : low + 2].astype(F32).reshape(1024, BLOCK)
    for arr, rows in enumerate((conv_rows, back_rows)):
        for m in range(OWN):
            part = turned[pl.ds(arr * OWN + m, 128, stride=8), :]
            rows.at[tile][pl.ds(m, BLOCK, stride=OWN), :] = part.T


def gradients(tile, conv_rows, back_rows, grad, key, value, out):
    lanes = pl.ds(128 * tile, 128)

    def body(k, carry):
        at = pl.ds(pl.multiple_of(16 * k, 16), 16)
        rows = pl.ds(pl.multiple_of(64 * k, 64), 64)
        conv = conv_rows[tile, rows, :].reshape(16, OWN, 128)
        back = back_rows[tile, rows, :].reshape(16, OWN, 128)
        out[0, at, :, lanes] = (grad[at, :, lanes].astype(F32) * conv).astype(BF16)
        out[1, at, :, lanes] = (back * value[at, :, lanes].astype(F32)).astype(BF16)
        out[2, at, :, lanes] = (back * key[at, :, lanes].astype(F32)).astype(BF16)
        return carry

    lax.fori_loop(0, BLOCK // 16, body, 0)


def toeplitz(taps, half, strip):
    strip[half, :, 0:128] = jnp.zeros((128, 128), BF16)

    def body(t, carry):
        now = taps[half, pl.ds(t, 1), :]
        before = taps[half, pl.ds(jnp.maximum(t - 1, 0), 1), :] * jnp.where(t > 0, 1.0, 0.0)
        both = jnp.broadcast_to(jnp.concatenate([before, now], axis=1), (128, 256))
        skewed = pltpu.roll(both, 0, 1, stride=1, stride_axis=0)
        at = pl.ds(pl.multiple_of(128 * (t + 1), 128), 128)
        strip[half, :, at] = skewed[:, 128:].astype(BF16)
        return carry

    lax.fori_loop(0, SEQ, body, 0, unroll=8)


def unpack(recv, half, mixed, gated):
    def body(j, carry):
        rows = pl.ds(pl.multiple_of(MEMBERS * j, MEMBERS), MEMBERS)
        for h in range(2):
            inputs, gates = [], []
            for c in (0, 2):
                low = recv[half, c, 2 * j + h].astype(F32)
                high = recv[half, c + 1, 2 * j + h].astype(F32)
                inputs.append(jnp.concatenate([low[:OWN], high[:OWN]], axis=0))
                gates.append(jnp.concatenate([low[OWN:], high[OWN:]], axis=0))
            lanes = slice(128 * h, 128 * h + 128)
            mixed[rows, lanes] = jnp.concatenate(inputs, axis=0).astype(BF16)
            gated[rows, lanes] = jnp.concatenate(gates, axis=0).astype(BF16)
        return carry

    lax.fori_loop(0, STEPS, body, 0, unroll=4)


def pack(conv, back, half, send):
    def body(i, carry):
        for h in range(2):
            lanes = slice(128 * h, 128 * h + 128)
            for c in (0, 2):
                rows = pl.ds(pl.multiple_of(MEMBERS * i + OWN * c, 8), 8)
                y = conv[rows, lanes]
                m = back[rows, lanes]
                send[half, c, 2 * i + h] = jnp.concatenate([y[:OWN], m[:OWN]], axis=0).astype(BF16)
                send[half, c + 1, 2 * i + h] = jnp.concatenate([y[OWN:], m[OWN:]], axis=0).astype(BF16)
        return carry

    lax.fori_loop(0, STEPS, body, 0, unroll=4)


def convolve(strip, half, mixed, gated, conv, back):
    for d in range(STEPS):
        o = PAIR * d
        weights = jnp.concatenate(
            [strip[half, :, o + 128 : o + 384], strip[half, :, o : o + 256]], axis=0
        )
        skip = MEMBERS * d
        y = dot(mixed[0 : ROWS - skip, :], weights)
        m = dot_rows(gated[skip:ROWS, :], weights)
        if d == 0:
            conv[...] = y
            back[...] = m
        else:
            conv[skip:ROWS, :] += y
            back[0 : ROWS - skip, :] += m


def lag(mixed, gated, half, flipped, outer, lags):
    row = lax.broadcasted_iota(jnp.int32, (PAIR, PAIR), 0)
    column = lax.broadcasted_iota(jnp.int32, (PAIR, PAIR), 1)
    eye = jnp.where(row == column, 1.0, 0.0).astype(BF16)
    flipped[...] = dot_rows(eye, mixed[...]).astype(BF16)
    outer[:, SEQ * BLOCK :] = jnp.zeros((PAIR, 256), F32)
    gated[ROWS:, :] = jnp.zeros((ROWS, PAIR), BF16)
    for d in range(STEPS):
        depth = ROWS if d < STEPS // 2 else ROWS // 2
        skip = MEMBERS * d
        outer[:, PAIR * d : PAIR * d + PAIR] = dot(
            flipped[:, :depth], gated[skip : skip + depth, :]
        )
    wide = 1024 + 128

    def chunk(n, carry):
        base = pl.multiple_of(1024 * n, 128)
        after = pl.multiple_of(base + 128, 128)

        def part(q):
            first = outer[8 * q : 8 * q + 8, pl.ds(base, wide)]
            return first + outer[128 + 8 * q : 136 + 8 * q, pl.ds(after, wide)]

        total = part(0)
        for q in range(1, 16):
            total = total + pltpu.roll(part(q), wide - 8 * q, 1)
        for step in (4, 2, 1):
            total = total + pltpu.roll(pltpu.roll(total, wide - step, 1), 8 - step, 0)
        for k in range(8):
            lags[half, 8 * n + k] = total[0:1, 128 * k : 128 * k + 128]
        return carry

    lax.fori_loop(0, SEQ * BLOCK // 1024, chunk, 0, unroll=4)


def partner(k, seq, ch):
    k = (k + 248) & 255
    turn = 7 - ((k >> 3) & 7)
    z = ((seq >> 1) + ((turn + 1) >> 1) * (2 * (turn & 1) - 1)) & 7
    far = k >> 6
    x = ((seq >> 4) + 2 - far - (far >> 1) - 2 * ((far >> 1) & far)) & 3
    return (x << 4) | (z << 1) | ((seq ^ (k >> 2)) & 1), ch ^ (k & 3)


def kernel(
    grad_hbm, query_hbm, key_hbm, value_hbm, filter_hbm,
    out, lag_out,
    grad, query, key, value, taps_in,
    mixed_rows, gated_rows, turned, taps_turned,
    taps_send, taps_recv, taps,
    send, recv, strip, mixed, gated, conv, back, flipped, outer,
    back_send, back_recv, lags, lag_recv,
    load_sem,
    taps_ssem, taps_rsem, send_sem, recv_sem, back_ssem, back_rsem, lag_ssem, lag_rsem,
):
    seq = lax.axis_index("seq")
    ch = lax.axis_index("ch")
    me = seq * CH + ch

    loads = [
        pltpu.make_async_copy(src, dst, load_sem.at[k])
        for k, (src, dst) in enumerate(
            ((key_hbm, key), (value_hbm, value), (grad_hbm, grad), (query_hbm, query), (filter_hbm, taps_in))
        )
    ]
    for load in loads:
        load.start()

    def remote(src, dst, ssem, rsem, target):
        return pltpu.make_async_remote_copy(
            src_ref=src,
            dst_ref=dst,
            send_sem=ssem,
            recv_sem=rsem,
            device_id=target,
            device_id_type=pl.DeviceIdType.LOGICAL,
        )

    barrier = pltpu.get_barrier_semaphore()

    far = 0b10100111

    def greet(k, carry):
        pl.semaphore_signal(
            barrier, inc=1, device_id=me ^ far ^ k, device_id_type=pl.DeviceIdType.LOGICAL
        )
        return carry

    lax.fori_loop(0, far, greet, 0, unroll=167)
    lax.fori_loop(far + 1, DEVICES, greet, 0, unroll=44)

    loads[0].wait()
    loads[1].wait()
    products(key, value, 0, mixed_rows)
    loads[2].wait()
    loads[3].wait()
    products(grad, query, 0, gated_rows)
    loads[4].wait()
    for half in range(2):
        lanes = pl.ds(pl.multiple_of(256 * half + 128 * (ch // 2), 128), 128)
        taps_turned[...] = taps_in[:, lanes].astype(F32).T
        picked = taps_turned[pl.ds(pl.multiple_of(64 * (ch % 2), 64), 64), :]
        taps_send[:, half, :] = picked.astype(BF16)
    for tile in (0, 1):
        spread(mixed_rows, gated_rows, tile, turned, send)

    pl.semaphore_wait(barrier, DEVICES - 1)

    pltpu.make_async_copy(taps_send.at[seq], taps_recv.at[seq], taps_rsem).start()

    def send_taps(k, carry):
        other = seq ^ (k + 1)
        remote(taps_send.at[other], taps_recv.at[seq], taps_ssem, taps_rsem, other * CH + ch).start()
        return carry

    lax.fori_loop(0, SEQ - 1, send_taps, 0, unroll=21)

    def exchange(src, dst, ssem, rsem):
        pltpu.make_async_copy(src.at[ch, seq], dst.at[ch, seq], rsem).start()

        def step(k, carry):
            other_seq, other_ch = partner(k + 1, seq, ch)
            target = other_seq * CH + other_ch
            remote(src.at[other_ch, other_seq], dst.at[ch, seq], ssem, rsem, target).start()
            return carry

        lax.fori_loop(0, DEVICES - 1, step, 0, unroll=51)

    exchange(send.at[0], recv.at[0], send_sem.at[0], recv_sem.at[0])
    products(key, value, 1, mixed_rows)
    products(grad, query, 1, gated_rows)
    for tile in (2, 3):
        spread(mixed_rows, gated_rows, tile, turned, send)
    exchange(send.at[1], recv.at[1], send_sem.at[1], recv_sem.at[1])

    pltpu.make_async_copy(taps_recv, taps_recv, taps_rsem).wait()
    for half in range(2):
        taps[half] = taps_recv[:, half, :].astype(F32)
        toeplitz(taps, half, strip)

    for half in range(2):
        pltpu.make_async_copy(recv.at[half], recv.at[half], recv_sem.at[half]).wait()
        unpack(recv, half, mixed, gated)
        convolve(strip, half, mixed, gated, conv, back)
        pack(conv, back, half, back_send)
        exchange(back_send.at[half], back_recv.at[half], back_ssem.at[half], back_rsem.at[half])
        lag(mixed, gated, half, flipped, outer, lags)
        lag_ch = 2 * half + ch // 2
        lag_slot = lag_recv.at[ch % 2, seq]

        @pl.when(lag_ch == ch)
        def _():
            pltpu.make_async_copy(lags.at[half, seq], lag_slot, lag_rsem).start()

        @pl.when(lag_ch != ch)
        def _():
            remote(lags.at[half, seq], lag_slot, lag_ssem, lag_rsem, seq * CH + lag_ch).start()

        def send_lags(k, carry):
            other = seq ^ (k + 1)
            remote(lags.at[half, other], lag_slot, lag_ssem, lag_rsem, other * CH + lag_ch).start()
            return carry

        lax.fori_loop(0, SEQ - 1, send_lags, 0, unroll=21)

    for half in range(2):
        pltpu.make_async_copy(back_recv.at[half], back_recv.at[half], back_rsem.at[half]).wait()
        for tile in (2 * half, 2 * half + 1):
            collect(back_recv, tile, turned, mixed_rows, gated_rows)
            gradients(tile, mixed_rows, gated_rows, grad, key, value, out)

    pltpu.make_async_copy(lag_recv, lag_recv, lag_rsem).wait()
    lag_out[...] = lag_recv[...].reshape(128, BLOCK).T * SCALE

    pltpu.make_async_copy(
        taps_send.at[pl.ds(0, SEQ - 1)], taps_send.at[pl.ds(0, SEQ - 1)], taps_ssem
    ).wait()
    for half in range(2):
        for buffer, sem in ((send, send_sem), (back_send, back_ssem)):
            for c in range(CH):
                piece = buffer.at[half, c, pl.ds(0, SEQ if c else SEQ - 1)]
                pltpu.make_async_copy(piece, piece, sem.at[half]).wait()

        sent = lags.at[half, pl.ds(0, SEQ - 1)]
        pltpu.make_async_copy(sent, sent, lag_ssem).wait()

        @pl.when(2 * half + ch // 2 != ch)
        def _():
            pltpu.make_async_copy(lags.at[half, 0], lags.at[half, 0], lag_ssem).wait()


def hand_over(out, lags, out_final, lag_final, sem):
    copies = [
        pltpu.make_async_copy(out.at[k, pl.ds(64 * h, 64)], out_final.at[k, pl.ds(64 * h, 64)], sem.at[2 * k + h])
        for k in range(3)
        for h in range(2)
    ]
    copies.append(pltpu.make_async_copy(lags, lag_final, sem.at[6]))
    for copy in copies:
        copy.start()
    for copy in copies:
        copy.wait()


def local(grad_output, query_act, key_act, value_act, long_filter):
    vmem = pltpu.VMEM
    dma = pltpu.SemaphoreType.DMA
    message = (2, CH, SEQ, 8, BLOCK)
    out, lags = pl.pallas_call(
        kernel,
        out_shape=(
            pltpu.VMEM((3, BLOCK, OWN, GROUPS), BF16),
            pltpu.VMEM((BLOCK, 128), F32),
        ),
        in_specs=[pl.BlockSpec(memory_space=pltpu.HBM)] * 5,
        out_specs=[pl.BlockSpec(memory_space=pltpu.VMEM)] * 2,
        scratch_shapes=[
            vmem((BLOCK, OWN, GROUPS), BF16),
            vmem((BLOCK, OWN, GROUPS), BF16),
            vmem((BLOCK, OWN, GROUPS), BF16),
            vmem((BLOCK, OWN, GROUPS), BF16),
            vmem((BLOCK, GROUPS), BF16),
            vmem((TILES, BLOCK * OWN, 128), F32),
            vmem((TILES, BLOCK * OWN, 128), F32),
            vmem((1024, BLOCK), F32),
            vmem((128, BLOCK), F32),
            vmem((SEQ, 2, BLOCK), BF16),
            vmem((SEQ, 2, BLOCK), BF16),
            vmem((2, SEQ, BLOCK), F32),
            vmem(message, BF16),
            vmem(message, BF16),
            vmem((2, 128, SEQ * BLOCK + 128), BF16),
            vmem((ROWS, PAIR), BF16),
            vmem((2 * ROWS, PAIR), BF16),
            vmem((ROWS, PAIR), F32),
            vmem((ROWS, PAIR), F32),
            vmem((PAIR, ROWS), BF16),
            vmem((PAIR, SEQ * BLOCK + 256), F32),
            vmem(message, BF16),
            vmem(message, BF16),
            vmem((2, SEQ, 1, BLOCK), F32),
            vmem((2, SEQ, 1, BLOCK), F32),
            dma((5,)),
            dma,
            dma,
            dma((2,)),
            dma((2,)),
            dma((2,)),
            dma((2,)),
            dma,
            dma,
        ],
        compiler_params=pltpu.CompilerParams(
            collective_id=0, has_side_effects=True, vmem_limit_bytes=56 * 2**20
        ),
        cost_estimate=pl.CostEstimate(
            flops=10_000_000_000, bytes_accessed=4_000_000, transcendentals=0
        ),
    )(grad_output, query_act, key_act, value_act, long_filter)
    return out, lags


def solution(mesh):
    wide = P("seq", "ch", None)
    in_specs = (wide, wide, wide, wide, P("seq", None))
    out_specs = (P(None, "seq", "ch", None), P("seq", "ch"))
    return jax.shard_map(local, mesh=mesh, in_specs=in_specs, out_specs=out_specs, check_vma=False)
```
